256 devices in a mesh: dp: 2 (over x_lo), ctx: 128 (over x_hi, y, z, core).
Axes of the slice: x: 4 (x_hi: 2, x_lo: 2; x = x_hi * 2 + x_lo), y: 4, z: 8, core: 2. Of those that a mesh axis runs over, the one named last changes fastest.
Arguments:
- features: bfloat16 [2, 16384, 1536], P('dp', 'ctx'), may hold values from -500 to 500
- gain: float32 [1536], replicated, may hold values from 0.1 to 1.9
- conv_weight: bfloat16 [5, 1536, 768], replicated, may hold values from -0.0625 to 0.0625
- cotangent: bfloat16 [2, 16384, 768], P('dp', 'ctx'), may hold values from -15 to 15
Outputs:
- convolved: bfloat16 [2, 16384, 768], P('dp', 'ctx')
- input_grad: bfloat16 [2, 16384, 1536], P('dp', 'ctx')
- gain_grad: float32 [1536], replicated
The draws below stay inside these ranges and needn't reach their ends.
All inputs are finite; a program needn't handle non-finite values.
Results may differ from the reference program's by a relative error of at most 0.0054.
Values may be sent and summed in bfloat16 or wider, within the bound.
No kernel may reach another device: no remote copies, remote signals or barrier semaphores. Data moves between devices by JAX's collectives and lax.ppermute only.
A program may use at most 64 MiB of HBM per device.

```python
import math
import jax
import jax.numpy as jnp
from jax import lax

CH = 1536
COUT = 768
KERNEL_TAPS = 5
LEN = 16384
DILATION_STEP = 2048
BATCH = 2


def draw_features(key, part):
    first_key, second_key, third_key = jax.random.split(jax.random.fold_in(key, 11), 3)
    base = jnp.clip(jax.random.normal(first_key, (BATCH, LEN, CH), jnp.float32), -5.0, 5.0)
    row_scale = jnp.exp(jax.random.uniform(second_key, (BATCH, LEN, 1), jnp.float32, 0.0, math.log(10.0)))
    column_scale = jnp.exp(jax.random.uniform(third_key, (1, 1, CH), jnp.float32, 0.0, math.log(10.0)))
    return (base * row_scale * column_scale).astype(jnp.bfloat16)


def draw_cotangent(key, part):
    first_key = jax.random.fold_in(jax.random.fold_in(key, 23), 0)
    position = jnp.arange(LEN, dtype=jnp.float32) / max(LEN - 1, 1)
    rising = jnp.exp(math.log(3.0) * position)
    base = jnp.clip(jax.random.normal(first_key, (BATCH, LEN, COUT), jnp.float32), -5.0, 5.0)
    return (base * rising[None, :, None]).astype(jnp.bfloat16)


def noise(own_key, shape, width, most, kind=jnp.bfloat16):
    return jnp.clip(width * jax.random.normal(own_key, shape, jnp.float32), -most, most).astype(kind)


def setup_inputs(seed: int = 0) -> dict:
    key_list = jax.random.split(jax.random.key(seed), 5)
    features = draw_features(jax.random.fold_in(key_list[4], 71), 0)
    gain = jnp.clip(1.0 + 0.18 * jax.random.normal(key_list[1], (CH,), jnp.float32), 0.1, 1.9)
    conv_weight = noise(key_list[2], (KERNEL_TAPS, CH, COUT), (KERNEL_TAPS * CH) ** -0.5, 0.0625)
    cotangent = draw_cotangent(jax.random.fold_in(key_list[4], 71), 0)
    return {"features": features, "gain": gain, "conv_weight": conv_weight, "cotangent": cotangent}


EPS = 1e-06

def activate(values):
    return jax.nn.gelu(values, approximate=True)

def shifted(values, strand_heading):
    reach_length = KERNEL_TAPS // 2 * DILATION_STEP
    padded = jnp.pad(values, ((0, 0), (reach_length, reach_length), (0, 0)))
    pieces = []
    for bin_displacement in range(KERNEL_TAPS):
        start_position = reach_length + strand_heading * (bin_displacement - KERNEL_TAPS // 2) * DILATION_STEP
        pieces.append(padded[:, start_position:start_position + LEN, :])
    return pieces

def apply_forward(pieces, weight):
    lead = pieces[0].shape[0]
    middle = pieces[0].shape[1]
    total = jnp.zeros((lead * middle, weight.shape[2]), jnp.float32)
    for tap_index in range(KERNEL_TAPS):
        flat_rows = pieces[tap_index].reshape(lead * middle, pieces[tap_index].shape[2])
        total = total + jnp.dot(flat_rows, weight[tap_index], preferred_element_type=jnp.float32)
    return total.reshape(lead, middle, weight.shape[2])

def apply_backward(pieces, weight):
    lead = pieces[0].shape[0]
    middle = pieces[0].shape[1]
    total = jnp.zeros((lead * middle, weight.shape[1]), jnp.float32)
    for tap_index in range(KERNEL_TAPS):
        flat_rows = pieces[tap_index].reshape(lead * middle, pieces[tap_index].shape[2])
        total = total + lax.dot_general(flat_rows, weight[tap_index], (((1,), (1,)), ((), ())), preferred_element_type=jnp.float32)
    return total.reshape(lead, middle, weight.shape[1])

def reference(features, gain, conv_weight, cotangent):
    wide = features.astype(jnp.float32)
    inv_rms = lax.rsqrt(lax.optimization_barrier(jnp.mean(wide * wide, axis=-1, keepdims=True)) + EPS)
    normed = wide * inv_rms
    scaled = normed * gain
    hidden = activate(scaled).astype(jnp.bfloat16)
    forward_term = apply_forward(shifted(hidden, 1), conv_weight)
    turned = apply_forward(shifted(hidden[:, ::-1, ::-1], 1), conv_weight).astype(jnp.bfloat16)
    reverse_term = turned[:, ::-1, ::-1]
    convolved = (forward_term + reverse_term.astype(jnp.float32)).astype(jnp.bfloat16)
    back_forward = apply_backward(shifted(cotangent, -1), conv_weight)
    back_turned = apply_backward(shifted(cotangent[:, ::-1, ::-1], -1), conv_weight).astype(jnp.bfloat16)
    grad_hidden = back_forward + back_turned[:, ::-1, ::-1].astype(jnp.float32)
    _, pullback = jax.vjp(activate, scaled)
    grad_scaled = pullback(grad_hidden)[0]
    gain_grad = lax.optimization_barrier(jnp.sum(grad_scaled * normed, axis=(0, 1))) / math.sqrt(BATCH * LEN)
    grad_normed = grad_scaled * gain
    spread_term = lax.optimization_barrier(jnp.mean(grad_normed * normed, axis=-1, keepdims=True))
    input_grad = (inv_rms * (grad_normed - normed * spread_term)).astype(jnp.bfloat16)
    return (convolved, input_grad, gain_grad)
```

```python
import math

import jax
import jax.numpy as jnp
from jax import lax
from jax.experimental import pallas as pl
from jax.experimental.pallas import tpu as pltpu
from jax.sharding import PartitionSpec as P

TAPS = 5
EPS = 1e-06
ROWS = 128
CH = 1536
COUT = 768
PART = 512
PARTS = CH // PART
TILE = 256
ROOT = math.sqrt(2.0 / math.pi)
CUBE = 0.044715
BF = jnp.bfloat16
F32 = jnp.float32


def exchange_matrix():
    rows = lax.broadcasted_iota(jnp.int32, (TILE, TILE), 0)
    cols = lax.broadcasted_iota(jnp.int32, (TILE, TILE), 1)
    return jnp.where(rows + cols == TILE - 1, 1.0, 0.0).astype(BF)


def flip_tile(ref, tile, count, swap, rows=slice(None)):
    first = (count - 1 - tile) * TILE
    return jnp.dot(ref[rows, first : first + TILE], swap, preferred_element_type=F32)


def fetch(weight, taps, buffer, sems):
    copies = []
    for slot, tap in enumerate(taps):
        for part in range(PARTS):
            rows = pl.ds(part * PART, PART)
            copy = pltpu.make_async_copy(
                weight.at[tap, rows], buffer.at[slot, rows], sems.at[slot, part]
            )
            copy.start()
            copies.append(copy)
    return copies


def partial_sums(stacked, buffer, sums, copies, count):
    for slot in range(count):
        for part in range(PARTS):
            copies[slot * PARTS + part].wait()
            span = slice(part * PART, (part + 1) * PART)
            term = jnp.dot(stacked[:, span], buffer[slot, span], preferred_element_type=F32)
            if part == 0:
                sums[slot] = term
            else:
                sums[slot] = sums[slot] + term


def forward_far_kernel(place, features, gain, weight, stacked, slope, inv_rms, to_a, to_b, buffer, sums, turned, sems):
    copies = fetch(weight, (0, 4), buffer, sems)
    wide = features[...].astype(F32)
    scale = lax.rsqrt(jnp.mean(wide * wide, axis=-1, keepdims=True) + EPS)
    inv_rms[...] = scale
    swap = exchange_matrix()
    scaled = wide * scale * gain[...]
    square = scaled * scaled
    bend = jnp.tanh(ROOT * (scaled + CUBE * (square * scaled)))
    stacked[:ROWS] = (0.5 * scaled * (1.0 + bend)).astype(BF)
    slope[...] = 0.5 * (1.0 + bend) + 0.5 * scaled * (1.0 - bend * bend) * (
        ROOT * (1.0 + 3.0 * CUBE * square)
    )
    for tile in range(CH // TILE):
        span = slice(tile * TILE, (tile + 1) * TILE)
        stacked[ROWS:, span] = flip_tile(stacked, tile, CH // TILE, swap, slice(0, ROWS)).astype(BF)
    partial_sums(stacked, buffer, sums, copies, 2)
    spot = place[0]
    even = lax.rem(spot, 2) == 0
    turned[...] = sums[:, ROWS:].astype(BF)
    ahead_ok = spot + 2 < 8
    behind_ok = spot - 2 >= 0
    for tile in range(COUT // TILE):
        span = slice(tile * TILE, (tile + 1) * TILE)
        ahead = sums[0, :ROWS, span] + flip_tile(turned.at[1], tile, COUT // TILE, swap)
        behind = sums[1, :ROWS, span] + flip_tile(turned.at[0], tile, COUT // TILE, swap)
        ahead = jnp.where(ahead_ok, ahead, 0.0).astype(BF)
        behind = jnp.where(behind_ok, behind, 0.0).astype(BF)

        @pl.when(even)
        def _(ahead=ahead, behind=behind, span=span):
            to_a[:, span] = ahead
            to_b[:, span] = behind

        @pl.when(jnp.logical_not(even))
        def _(ahead=ahead, behind=behind, span=span):
            to_a[:, span] = behind
            to_b[:, span] = ahead


def forward_near_kernel(place, stacked, from_a, from_b, weight, to_a, to_b, own, buffer, sums, turned, sems):
    copies = fetch(weight, (1, 3, 2), buffer, sems)
    swap = exchange_matrix()
    partial_sums(stacked, buffer, sums, copies, 3)
    spot = place[0]
    even = lax.rem(spot, 2) == 0
    turned[...] = sums[:, ROWS:].astype(BF)
    ahead_ok = spot + 1 < 8
    behind_ok = spot - 1 >= 0
    for tile in range(COUT // TILE):
        span = slice(tile * TILE, (tile + 1) * TILE)
        ahead = sums[0, :ROWS, span] + flip_tile(turned.at[1], tile, COUT // TILE, swap)
        behind = sums[1, :ROWS, span] + flip_tile(turned.at[0], tile, COUT // TILE, swap)
        ahead = jnp.where(ahead_ok, ahead, 0.0)
        behind = jnp.where(behind_ok, behind, 0.0)
        own[:, span] = sums[2, :ROWS, span] + flip_tile(turned.at[2], tile, COUT // TILE, swap)

        @pl.when(even)
        def _(ahead=ahead, behind=behind, span=span):
            to_a[:, span] = (ahead + from_b[:, span].astype(F32)).astype(BF)
            to_b[:, span] = (behind + from_a[:, span].astype(F32)).astype(BF)

        @pl.when(jnp.logical_not(even))
        def _(ahead=ahead, behind=behind, span=span):
            to_a[:, span] = (behind + from_b[:, span].astype(F32)).astype(BF)
            to_b[:, span] = (ahead + from_a[:, span].astype(F32)).astype(BF)


def join_kernel(own, from_a, from_b, convolved):
    convolved[...] = (own[...] + (from_a[...].astype(F32) + from_b[...].astype(F32))).astype(BF)


def stack_pair(lhs, even, ok_ahead, ok_behind, first, second, tap_low, tap_high, swap):
    zero = jnp.zeros((ROWS, COUT), BF)
    for flag, ahead_ref, behind_ref in ((True, first, second), (False, second, first)):

        @pl.when(even if flag else jnp.logical_not(even))
        def _(ahead_ref=ahead_ref, behind_ref=behind_ref):
            lhs[tap_low, :ROWS] = jnp.where(ok_ahead, ahead_ref[...], zero)
            lhs[tap_high, :ROWS] = jnp.where(ok_behind, behind_ref[...], zero)

    for tile in range(COUT // TILE):
        span = slice(tile * TILE, (tile + 1) * TILE)
        lhs[tap_low, ROWS:, span] = flip_tile(lhs.at[tap_high], tile, COUT // TILE, swap, slice(0, ROWS)).astype(BF)
        lhs[tap_high, ROWS:, span] = flip_tile(lhs.at[tap_low], tile, COUT // TILE, swap, slice(0, ROWS)).astype(BF)


def pull_back(lhs, buffer, total, copies, count, fresh):
    for slot in range(count):
        for part in range(PARTS):
            copies[slot * PARTS + part].wait()
            span = slice(part * PART, (part + 1) * PART)
            term = lax.dot_general(
                lhs[slot],
                buffer[slot, span],
                (((1,), (1,)), ((), ())),
                preferred_element_type=F32,
            )
            if slot == 0 and fresh:
                total[:, span] = term
            else:
                total[:, span] = total[:, span] + term


def backward_near_kernel(place, own, from_a, from_b, weight, total, buffer, lhs, sems):
    copies = fetch(weight, (2, 1, 3), buffer, sems)
    swap = exchange_matrix()
    spot = place[0]
    even = lax.rem(spot, 2) == 0
    lhs[0, :ROWS] = own[...]
    for tile in range(COUT // TILE):
        span = slice(tile * TILE, (tile + 1) * TILE)
        lhs[0, ROWS:, span] = flip_tile(own, tile, COUT // TILE, swap).astype(BF)
    stack_pair(lhs, even, spot + 1 < 8, spot - 1 >= 0, from_a, from_b, 1, 2, swap)
    pull_back(lhs, buffer, total, copies, 3, True)


def backward_far_kernel(
    place, from_a, from_b, weight, near, features, gain, slope, inv_rms, grad, gain_part, total, buffer, lhs, turned, sems
):
    copies = fetch(weight, (0, 4), buffer, sems)
    swap = exchange_matrix()
    spot = place[0]
    even = lax.rem(spot, 2) == 0
    stack_pair(lhs, even, spot + 2 < 8, spot - 2 >= 0, from_a, from_b, 0, 1, swap)
    total[...] = near[...]
    pull_back(lhs, buffer, total, copies, 2, False)
    turned[...] = total[ROWS:].astype(BF)
    scale = inv_rms[...]
    spread = jnp.zeros((ROWS, 1), F32)
    for tile in range(CH // TILE):
        span = slice(tile * TILE, (tile + 1) * TILE)
        hidden_grad = total[:ROWS, span] + flip_tile(turned, tile, CH // TILE, swap)
        scaled_grad = hidden_grad * slope[:, span]
        product = scaled_grad * (features[:, span].astype(F32) * scale)
        gain_part[:, span] = jnp.sum(product, axis=0, keepdims=True)
        spread = spread + jnp.sum(product * gain[:, span], axis=-1, keepdims=True)
        total[:ROWS, span] = scaled_grad * gain[:, span]
    spread = spread * (1.0 / CH)
    normed = features[...].astype(F32) * scale
    grad[...] = (scale * (total[:ROWS] - normed * spread)).astype(BF)


VMEM = pl.BlockSpec(memory_space=pltpu.VMEM)
SMEM = pl.BlockSpec(memory_space=pltpu.SMEM)
HBM = pl.BlockSpec(memory_space=pl.ANY)
LIMIT = pltpu.CompilerParams(vmem_limit_bytes=56 * 2**20)


def shape(dims, kind):
    return jax.ShapeDtypeStruct(dims, kind)


def forward_far(place, features, gain, weight):
    return pl.pallas_call(
        forward_far_kernel,
        out_shape=(
            shape((2 * ROWS, CH), BF),
            shape((ROWS, CH), F32),
            shape((ROWS, 1), F32),
            shape((ROWS, COUT), BF),
            shape((ROWS, COUT), BF),
        ),
        in_specs=[SMEM, VMEM, VMEM, HBM],
        out_specs=[VMEM] * 5,
        scratch_shapes=[
            pltpu.VMEM((2, CH, COUT), BF),
            pltpu.VMEM((2, 2 * ROWS, COUT), F32),
            pltpu.VMEM((2, ROWS, COUT), BF),
            pltpu.SemaphoreType.DMA((2, PARTS)),
        ],
        compiler_params=LIMIT,
        cost_estimate=pl.CostEstimate(flops=1300000000, bytes_accessed=7000000, transcendentals=200000),
        name="forward_far",
    )(place, features, gain, weight)


def forward_near(place, stacked, from_a, from_b, weight):
    return pl.pallas_call(
        forward_near_kernel,
        out_shape=(
            shape((ROWS, COUT), BF),
            shape((ROWS, COUT), BF),
            shape((ROWS, COUT), F32),
        ),
        in_specs=[SMEM, VMEM, VMEM, VMEM, HBM],
        out_specs=[VMEM] * 3,
        scratch_shapes=[
            pltpu.VMEM((3, CH, COUT), BF),
            pltpu.VMEM((3, 2 * ROWS, COUT), F32),
            pltpu.VMEM((3, ROWS, COUT), BF),
            pltpu.SemaphoreType.DMA((3, PARTS)),
        ],
        compiler_params=LIMIT,
        cost_estimate=pl.CostEstimate(flops=1900000000, bytes_accessed=9000000, transcendentals=0),
        name="forward_near",
    )(place, stacked, from_a, from_b, weight)


def join(own, from_a, from_b):
    return pl.pallas_call(
        join_kernel,
        out_shape=shape((ROWS, COUT), BF),
        in_specs=[VMEM] * 3,
        out_specs=VMEM,
        cost_estimate=pl.CostEstimate(flops=200000, bytes_accessed=1000000, transcendentals=0),
        name="join",
    )(own, from_a, from_b)


def backward_near(place, own, from_a, from_b, weight):
    return pl.pallas_call(
        backward_near_kernel,
        out_shape=shape((2 * ROWS, CH), F32),
        in_specs=[SMEM, VMEM, VMEM, VMEM, HBM],
        out_specs=VMEM,
        scratch_shapes=[
            pltpu.VMEM((3, CH, COUT), BF),
            pltpu.VMEM((3, 2 * ROWS, COUT), BF),
            pltpu.SemaphoreType.DMA((3, PARTS)),
        ],
        compiler_params=LIMIT,
        cost_estimate=pl.CostEstimate(flops=1900000000, bytes_accessed=9000000, transcendentals=0),
        name="backward_near",
    )(place, own, from_a, from_b, weight)


def backward_far(place, from_a, from_b, weight, near, features, gain, slope, inv_rms):
    return pl.pallas_call(
        backward_far_kernel,
        out_shape=(shape((ROWS, CH), BF), shape((1, CH), F32)),
        in_specs=[SMEM, VMEM, VMEM, HBM, VMEM, VMEM, VMEM, VMEM, VMEM],
        out_specs=[VMEM] * 2,
        scratch_shapes=[
            pltpu.VMEM((2 * ROWS, CH), F32),
            pltpu.VMEM((2, CH, COUT), BF),
            pltpu.VMEM((2, 2 * ROWS, COUT), BF),
            pltpu.VMEM((ROWS, CH), BF),
            pltpu.SemaphoreType.DMA((2, PARTS)),
        ],
        compiler_params=LIMIT,
        cost_estimate=pl.CostEstimate(flops=1300000000, bytes_accessed=7000000, transcendentals=0),
        name="backward_far",
    )(place, from_a, from_b, weight, near, features, gain, slope, inv_rms)


def exchange_a(value):
    return lax.ppermute(value, "ctx", [(i, ((i // 16) ^ 1) * 16 + i % 16) for i in range(128)])


def exchange_b(value):
    pairs = []
    for i in range(128):
        spot = i // 16
        other = (spot + 1) % 8 if spot % 2 else (spot - 1) % 8
        pairs.append((i, other * 16 + i % 16))
    return lax.ppermute(value, "ctx", pairs)


BOTH = ("dp", "ctx")


def turn(value, base, radix, step):
    pairs = []
    for i in range(256):
        digit = (i // base) % radix
        pairs.append((i, i + ((digit + step) % radix - digit) * base))
    return lax.ppermute(value, BOTH, pairs)


def sum_everywhere(value):
    for base, radix in ((1, 4), (4, 4), (16, 4), (64, 4)):
        others = [turn(value, base, radix, step) for step in range(1, radix)]
        for other in others:
            value = value + other
    return value


def per_device(features, gain, conv_weight, cotangent):
    spot = (lax.axis_index("ctx") // 16).astype(jnp.int32)
    place = spot.reshape(1)
    rows = features.reshape(ROWS, CH)
    gain_row = gain.reshape(1, CH)
    own = cotangent.reshape(ROWS, COUT)
    grad_a = exchange_a(own)
    grad_b = exchange_b(own)
    stacked, slope, inv_rms, to_a, to_b = forward_far(place, rows, gain_row, conv_weight)
    grad_ba = exchange_a(grad_b)
    grad_ab = exchange_b(grad_a)
    near = backward_near(place, own, grad_a, grad_b, conv_weight)
    input_grad, gain_part = backward_far(
        place, grad_ba, grad_ab, conv_weight, near, rows, gain_row, slope, inv_rms
    )
    far_a = exchange_a(to_a)
    far_b = exchange_b(to_b)
    near_a, near_b, own_term = forward_near(place, stacked, far_a, far_b, conv_weight)
    convolved = join(own_term, exchange_a(near_a), exchange_b(near_b))
    summed = sum_everywhere(gain_part)
    total_rows = 2 * 16384
    gain_grad = summed.reshape(CH) / math.sqrt(total_rows)
    return (
        convolved.reshape(1, ROWS, COUT),
        input_grad.reshape(1, ROWS, CH),
        gain_grad,
    )


def solution(mesh):
    return jax.shard_map(
        per_device,
        mesh=mesh,
        in_specs=(P("dp", "ctx", None), P(), P(), P("dp", "ctx", None)),
        out_specs=(P("dp", "ctx", None), P("dp", "ctx", None), P()),
        check_vma=False,
    )
```

```python
import math

import jax
import jax.numpy as jnp
from jax import lax
from jax.experimental import pallas as pl
from jax.experimental.pallas import tpu as pltpu
from jax.sharding import PartitionSpec as P

TAPS = 5
EPS = 1e-06
ROWS = 128
CH = 1536
COUT = 768
PART = 768
PARTS = CH // PART
TILE = 256
ROOT = math.sqrt(2.0 / math.pi)
CUBE = 0.044715
FAR = (0, 4)
LANES = 128
PART_OUT = 512
BF = jnp.bfloat16
F32 = jnp.float32


def exchange_matrix():
    rows = lax.broadcasted_iota(jnp.int32, (TILE, TILE), 0)
    cols = lax.broadcasted_iota(jnp.int32, (TILE, TILE), 1)
    return jnp.where(rows + cols == TILE - 1, 1.0, 0.0).astype(BF)


def flip_tile(ref, tile, count, swap, rows=slice(None)):
    first = (count - 1 - tile) * TILE
    return jnp.dot(ref[rows, first : first + TILE], swap, preferred_element_type=F32)


def fetch(weight, taps, held, sems):
    copies = []
    for slot, tap in enumerate(taps):
        for part in range(PARTS):
            rows = pl.ds(part * PART, PART)
            copy = pltpu.make_async_copy(weight.at[tap, rows], held.at[slot, rows], sems.at[slot, part])
            copy.start()
            copies.append(copy)
    return copies


def partial_sums(stacked, held, sums, turned, slots):
    for place, slot in enumerate(slots):
        product = jnp.dot(stacked[...], held[slot], preferred_element_type=F32)
        sums[place] = product[:ROWS]
        turned[place] = product[ROWS:].astype(BF)


def outgoing(sums, turned, swap, spot, reach, to_a, to_b):
    even = lax.rem(spot, 2) == 0
    ahead_ok = spot + reach < 8
    behind_ok = spot - reach >= 0
    for tile in range(COUT // TILE):
        span = slice(tile * TILE, (tile + 1) * TILE)
        ahead = sums[0, :, span] + flip_tile(turned.at[1], tile, COUT // TILE, swap)
        behind = sums[1, :, span] + flip_tile(turned.at[0], tile, COUT // TILE, swap)
        ahead = jnp.where(ahead_ok, ahead, 0.0)
        behind = jnp.where(behind_ok, behind, 0.0)
        to_a[:, span] = jnp.where(even, ahead, behind).astype(to_a.dtype)
        to_b[:, span] = jnp.where(even, behind, ahead).astype(to_b.dtype)


def first_kernel(
    place, source, gain, weight, held, stacked, normed, slope, inv_rms, far_a, far_b, features, sums, turned, row_sem, sems
):
    load = pltpu.make_async_copy(source, features, row_sem)
    load.start()
    copies = fetch(weight, FAR, held, sems)
    swap = exchange_matrix()
    load.wait()
    wide = features[...].astype(F32)
    scale = lax.rsqrt(jnp.mean(wide * wide, axis=-1, keepdims=True) + EPS)
    inv_rms[...] = scale
    for lane in range(CH // LANES):
        span = slice(lane * LANES, (lane + 1) * LANES)
        value = features[:, span].astype(F32) * scale
        normed[:, span] = value
        scaled = value * gain[lane : lane + 1]
        square = scaled * scaled
        bend = jnp.tanh(ROOT * (scaled + CUBE * (square * scaled)))
        stacked[:ROWS, span] = (0.5 * scaled * (1.0 + bend)).astype(BF)
        slope[:, span] = 0.5 * (1.0 + bend) + 0.5 * scaled * (1.0 - bend * bend) * (
            ROOT * (1.0 + 3.0 * CUBE * square)
        )
    for tile in range(CH // TILE):
        span = slice(tile * TILE, (tile + 1) * TILE)
        stacked[ROWS:, span] = flip_tile(stacked, tile, CH // TILE, swap, slice(0, ROWS)).astype(BF)
    for copy in copies:
        copy.wait()
    partial_sums(stacked, held, sums, turned, (0, 1))
    outgoing(sums, turned, swap, place[0], 2, far_a, far_b)


def middle_kernel(place, stacked, weight, grad, grad_a, grad_b, near_a, near_b, own, total, sums, turned, lhs):
    swap = exchange_matrix()
    spot = place[0]
    even = lax.rem(spot, 2) == 0
    lhs[1, :ROWS] = grad[...]
    for tile in range(COUT // TILE):
        span = slice(tile * TILE, (tile + 1) * TILE)
        lhs[1, ROWS:, span] = flip_tile(grad, tile, COUT // TILE, swap).astype(BF)
    stack_pair(lhs, even, spot + 1 < 8, spot - 1 >= 0, grad_a, grad_b, 0, 2, swap)
    partial_sums(stacked, weight, sums, turned, (2,))
    for tile in range(COUT // TILE):
        span = slice(tile * TILE, (tile + 1) * TILE)
        own[:, span] = sums[0, :, span] + flip_tile(turned.at[0], tile, COUT // TILE, swap)
    partial_sums(stacked, weight, sums, turned, (1, 3))
    outgoing(sums, turned, swap, spot, 1, near_a, near_b)
    for part in range(CH // PART_OUT):
        span = slice(part * PART_OUT, (part + 1) * PART_OUT)
        total[:, span] = (
            pull_back(lhs[0], weight[1, span])
            + pull_back(lhs[1], weight[2, span])
            + pull_back(lhs[2], weight[3, span])
        )


def relay_kernel(near_a, near_b, from_a, from_b, to_a, to_b):
    to_a[...] = (near_a[...] + from_b[...].astype(F32)).astype(BF)
    to_b[...] = (near_b[...] + from_a[...].astype(F32)).astype(BF)


def join_kernel(own, from_a, from_b, convolved):
    convolved[...] = (own[...] + (from_a[...].astype(F32) + from_b[...].astype(F32))).astype(BF)


def stack_pair(lhs, even, ok_ahead, ok_behind, first, second, tap_low, tap_high, swap):
    zero = jnp.zeros((ROWS, COUT), BF)
    for flag, ahead_ref, behind_ref in ((True, first, second), (False, second, first)):

        @pl.when(even if flag else jnp.logical_not(even))
        def _(ahead_ref=ahead_ref, behind_ref=behind_ref):
            lhs[tap_low, :ROWS] = jnp.where(ok_ahead, ahead_ref[...], zero)
            lhs[tap_high, :ROWS] = jnp.where(ok_behind, behind_ref[...], zero)

    for tile in range(COUT // TILE):
        span = slice(tile * TILE, (tile + 1) * TILE)
        lhs[tap_low, ROWS:, span] = flip_tile(lhs.at[tap_high], tile, COUT // TILE, swap, slice(0, ROWS)).astype(BF)
        lhs[tap_high, ROWS:, span] = flip_tile(lhs.at[tap_low], tile, COUT // TILE, swap, slice(0, ROWS)).astype(BF)


def pull_back(rows, weight):
    return lax.dot_general(rows, weight, (((1,), (1,)), ((), ())), preferred_element_type=F32)


def last_kernel(place, from_a, from_b, held, near, normed, gain, slope, inv_rms, grad, gain_part, total, lhs, turned):
    swap = exchange_matrix()
    spot = place[0]
    even = lax.rem(spot, 2) == 0
    stack_pair(lhs, even, spot + 2 < 8, spot - 2 >= 0, from_a, from_b, 0, 1, swap)
    for part in range(CH // PART_OUT):
        span = slice(part * PART_OUT, (part + 1) * PART_OUT)
        term = near[:, span] + pull_back(lhs[0], held[0, span]) + pull_back(lhs[1], held[1, span])
        total[:, span] = term[:ROWS]
        turned[:, span] = term[ROWS:].astype(BF)
    spread = jnp.zeros((ROWS, 1), F32)
    for tile in range(CH // TILE):
        flipped = flip_tile(turned, tile, CH // TILE, swap)
        for half in range(TILE // LANES):
            lane = tile * (TILE // LANES) + half
            span = slice(lane * LANES, (lane + 1) * LANES)
            hidden_grad = total[:, span] + flipped[:, half * LANES : (half + 1) * LANES]
            scaled_grad = hidden_grad * slope[:, span]
            product = scaled_grad * normed[:, span]
            gain_part[lane : lane + 1] = jnp.sum(product, axis=0, keepdims=True)
            spread = spread + jnp.sum(product * gain[lane : lane + 1], axis=-1, keepdims=True)
            total[:, span] = scaled_grad * gain[lane : lane + 1]
    spread = spread * (1.0 / CH)
    scale = inv_rms[...]
    for tile in range(CH // TILE):
        span = slice(tile * TILE, (tile + 1) * TILE)
        grad[:, span] = (scale * (total[:, span] - normed[:, span] * spread)).astype(BF)


VMEM = pl.BlockSpec(memory_space=pltpu.VMEM)
SMEM = pl.BlockSpec(memory_space=pltpu.SMEM)
HBM = pl.BlockSpec(memory_space=pl.ANY)
LIMIT = pltpu.CompilerParams(vmem_limit_bytes=24 * 2**20)


def shape(dims, kind):
    return jax.ShapeDtypeStruct(dims, kind)


def remote(value):
    return pltpu.with_memory_space_constraint(value, pltpu.HBM)


def local(value):
    return pltpu.with_memory_space_constraint(value, pltpu.VMEM)


def first(place, features, gain, weight):
    return pl.pallas_call(
        first_kernel,
        out_shape=(
            pltpu.VMEM((2, CH, COUT), BF),
            pltpu.VMEM((2 * ROWS, CH), BF),
            pltpu.VMEM((ROWS, CH), F32),
            pltpu.VMEM((ROWS, CH), F32),
            pltpu.VMEM((ROWS, 1), F32),
            pltpu.VMEM((ROWS, COUT), BF),
            pltpu.VMEM((ROWS, COUT), BF),
        ),
        in_specs=[SMEM, HBM, VMEM, HBM],
        out_specs=[VMEM] * 7,
        scratch_shapes=[
            pltpu.VMEM((ROWS, CH), BF),
            pltpu.VMEM((2, ROWS, COUT), F32),
            pltpu.VMEM((2, ROWS, COUT), BF),
            pltpu.SemaphoreType.DMA,
            pltpu.SemaphoreType.DMA((2, PARTS)),
        ],
        compiler_params=LIMIT,
        cost_estimate=pl.CostEstimate(flops=1300000000, bytes_accessed=6000000, transcendentals=200000),
        name="first",
    )(place, remote(features), local(gain), remote(weight))


def middle(place, stacked, weight, grad, grad_a, grad_b):
    return pl.pallas_call(
        middle_kernel,
        out_shape=(
            pltpu.VMEM((ROWS, COUT), F32),
            pltpu.VMEM((ROWS, COUT), F32),
            pltpu.VMEM((ROWS, COUT), F32),
            pltpu.VMEM((2 * ROWS, CH), F32),
        ),
        in_specs=[SMEM] + [VMEM] * 5,
        out_specs=[VMEM] * 4,
        scratch_shapes=[
            pltpu.VMEM((2, ROWS, COUT), F32),
            pltpu.VMEM((2, ROWS, COUT), BF),
            pltpu.VMEM((3, 2 * ROWS, COUT), BF),
        ],
        compiler_params=LIMIT,
        cost_estimate=pl.CostEstimate(flops=3600000000, bytes_accessed=8000000, transcendentals=0),
        name="middle",
    )(place, local(stacked), local(weight), local(grad), local(grad_a), local(grad_b))


def last(place, from_a, from_b, held, near, normed, gain, slope, inv_rms):
    return pl.pallas_call(
        last_kernel,
        out_shape=(shape((ROWS, CH), BF), pltpu.VMEM((CH // LANES, LANES), F32)),
        in_specs=[SMEM] + [VMEM] * 8,
        out_specs=[VMEM] * 2,
        scratch_shapes=[
            pltpu.VMEM((ROWS, CH), F32),
            pltpu.VMEM((2, 2 * ROWS, COUT), BF),
            pltpu.VMEM((ROWS, CH), BF),
        ],
        compiler_params=LIMIT,
        cost_estimate=pl.CostEstimate(flops=1300000000, bytes_accessed=1000000, transcendentals=0),
        name="last",
    )(place, *(local(value) for value in (from_a, from_b, held, near, normed, gain, slope, inv_rms)))


def relay(near_a, near_b, from_a, from_b):
    return pl.pallas_call(
        relay_kernel,
        out_shape=(pltpu.VMEM((ROWS, COUT), BF), pltpu.VMEM((ROWS, COUT), BF)),
        in_specs=[VMEM] * 4,
        out_specs=[VMEM] * 2,
        compiler_params=LIMIT,
        cost_estimate=pl.CostEstimate(flops=400000, bytes_accessed=1000000, transcendentals=0),
        name="relay",
    )(local(near_a), local(near_b), local(from_a), local(from_b))


def join(own, from_a, from_b):
    return pl.pallas_call(
        join_kernel,
        out_shape=shape((ROWS, COUT), BF),
        in_specs=[VMEM] * 3,
        out_specs=VMEM,
        compiler_params=LIMIT,
        cost_estimate=pl.CostEstimate(flops=200000, bytes_accessed=1000000, transcendentals=0),
        name="join",
    )(local(own), local(from_a), local(from_b))


def exchange_a(value):
    return lax.ppermute(value, "ctx", [(i, ((i // 16) ^ 1) * 16 + i % 16) for i in range(128)])


def exchange_b(value):
    pairs = []
    for i in range(128):
        spot = i // 16
        other = (spot + 1) % 8 if spot % 2 else (spot - 1) % 8
        pairs.append((i, other * 16 + i % 16))
    return lax.ppermute(value, "ctx", pairs)


BOTH = ("dp", "ctx")
DIGITS = {"core": (1, 2), "z": (2, 8), "y": (16, 4), "xh": (64, 2), "xl": (128, 2)}


def turn(value, **steps):
    pairs = []
    for i in range(256):
        target = i
        for name, step in steps.items():
            base, radix = DIGITS[name]
            digit = (i // base) % radix
            target += ((digit + step) % radix - digit) * base
        pairs.append((i, target))
    return lax.ppermute(value, BOTH, pairs)


def sum_everywhere(value):
    value = value + turn(value, core=1)
    low = turn(value, z=1)
    high = turn(value, z=-1)
    pair = value + high
    three = pair + low
    value = three + turn(three, z=3) + turn(pair, z=-2)
    value = value + turn(value, xl=1) + turn(value, xh=1) + turn(value, xl=1, xh=1)
    return value + turn(value, y=1) + turn(value, y=2) + turn(value, y=-1)


def per_device(features, gain, conv_weight, cotangent):
    spot = (lax.axis_index("ctx") // 16).astype(jnp.int32)
    place = spot.reshape(1)
    rows = features.reshape(ROWS, CH)
    gains = gain.reshape(CH // LANES, LANES)
    own = cotangent.reshape(ROWS, COUT)
    grad_a = exchange_a(own)
    grad_b = exchange_b(own)
    held, stacked, normed, slope, inv_rms, far_a, far_b = first(place, rows, gains, conv_weight)
    grad_a, grad_b, held = lax.optimization_barrier((grad_a, grad_b, held))
    grad_ba = exchange_a(grad_b)
    grad_ab = exchange_b(grad_a)
    near_a, near_b, center, near = middle(place, stacked, conv_weight, own, grad_a, grad_b)
    input_grad, gain_part = last(place, grad_ba, grad_ab, held, near, normed, gains, slope, inv_rms)
    to_a, to_b = relay(near_a, near_b, exchange_a(far_a), exchange_b(far_b))
    convolved = join(center, exchange_a(to_a), exchange_b(to_b))
    gain_grad = sum_everywhere(gain_part).reshape(CH) / math.sqrt(2 * 16384)
    return (
        convolved.reshape(1, ROWS, COUT),
        input_grad.reshape(1, ROWS, CH),
        gain_grad,
    )


def solution(mesh):
    return jax.shard_map(
        per_device,
        mesh=mesh,
        in_specs=(P("dp", "ctx", None), P(), P(), P("dp", "ctx", None)),
        out_specs=(P("dp", "ctx", None), P("dp", "ctx", None), P()),
        check_vma=False,
    )
```

```python
import math

import jax
import jax.numpy as jnp
from jax import lax
from jax.experimental import pallas as pl
from jax.experimental.pallas import tpu as pltpu
from jax.sharding import PartitionSpec as P

TAPS = 5
EPS = 1e-06
ROWS = 128
CH = 1536
COUT = 768
PART = 768
PARTS = CH // PART
TILE = 256
ROOT = math.sqrt(2.0 / math.pi)
CUBE = 0.044715
FAR = (0, 4)
LANES = 128
GROUP = 16
PART_OUT = 512
BF = jnp.bfloat16
F32 = jnp.float32


def exchange_matrix():
    rows = lax.broadcasted_iota(jnp.int32, (TILE, TILE), 0)
    cols = lax.broadcasted_iota(jnp.int32, (TILE, TILE), 1)
    return jnp.where(rows + cols == TILE - 1, 1.0, 0.0).astype(BF)


def flip_tile(ref, tile, count, swap, rows=slice(None)):
    first = (count - 1 - tile) * TILE
    return jnp.dot(ref[rows, first : first + TILE], swap, preferred_element_type=F32)


def fetch(weight, taps, held, sems):
    copies = []
    for slot, tap in enumerate(taps):
        for part in range(PARTS):
            rows = pl.ds(part * PART, PART)
            copy = pltpu.make_async_copy(weight.at[tap, rows], held.at[slot, rows], sems.at[slot, part])
            copy.start()
            copies.append(copy)
    return copies


def partial_sums(stacked, held, sums, turned, slots):
    for place, slot in enumerate(slots):
        product = jnp.dot(stacked[...], held[slot], preferred_element_type=F32)
        sums[place] = product[:ROWS]
        turned[place] = product[ROWS:].astype(BF)


def outgoing(sums, turned, swap, spot, reach, to_a, to_b):
    even = lax.rem(spot, 2) == 0
    ahead_ok = spot + reach < 8
    behind_ok = spot - reach >= 0
    for tile in range(COUT // TILE):
        span = slice(tile * TILE, (tile + 1) * TILE)
        ahead = sums[0, :, span] + flip_tile(turned.at[1], tile, COUT // TILE, swap)
        behind = sums[1, :, span] + flip_tile(turned.at[0], tile, COUT // TILE, swap)
        ahead = jnp.where(ahead_ok, ahead, 0.0)
        behind = jnp.where(behind_ok, behind, 0.0)
        to_a[:, span] = jnp.where(even, ahead, behind).astype(to_a.dtype)
        to_b[:, span] = jnp.where(even, behind, ahead).astype(to_b.dtype)


def first_kernel(
    place,
    source,
    gain_source,
    weight,
    held,
    stacked,
    normed,
    slope,
    inv_rms,
    far_a,
    far_b,
    gain,
    features,
    sums,
    turned,
    row_sem,
    gain_sem,
    sems,
):
    load = pltpu.make_async_copy(source, features, row_sem)
    load.start()
    gain_load = pltpu.make_async_copy(gain_source, gain, gain_sem)
    gain_load.start()
    copies = fetch(weight, FAR, held, sems)
    swap = exchange_matrix()
    load.wait()
    wide = features[...].astype(F32)
    scale = lax.rsqrt(jnp.mean(wide * wide, axis=-1, keepdims=True) + EPS)
    inv_rms[...] = scale
    gain_load.wait()
    for lane in range(CH // LANES):
        span = slice(lane * LANES, (lane + 1) * LANES)
        value = features[:, span].astype(F32) * scale
        normed[:, span] = value
        scaled = value * gain[lane : lane + 1]
        square = scaled * scaled
        bend = jnp.tanh(ROOT * (scaled + CUBE * (square * scaled)))
        stacked[:ROWS, span] = (0.5 * scaled * (1.0 + bend)).astype(BF)
        slope[:, span] = 0.5 * (1.0 + bend) + 0.5 * scaled * (1.0 - bend * bend) * (
            ROOT * (1.0 + 3.0 * CUBE * square)
        )
    for tile in range(CH // TILE):
        span = slice(tile * TILE, (tile + 1) * TILE)
        stacked[ROWS:, span] = flip_tile(stacked, tile, CH // TILE, swap, slice(0, ROWS)).astype(BF)
    for copy in copies:
        copy.wait()
    partial_sums(stacked, held, sums, turned, (0, 1))
    outgoing(sums, turned, swap, place[0], 2, far_a, far_b)


def ahead_kernel(place, stacked, weight, near_a, near_b, own, sums, turned):
    swap = exchange_matrix()
    partial_sums(stacked, weight, sums, turned, (2,))
    for tile in range(COUT // TILE):
        span = slice(tile * TILE, (tile + 1) * TILE)
        own[:, span] = sums[0, :, span] + flip_tile(turned.at[0], tile, COUT // TILE, swap)
    partial_sums(stacked, weight, sums, turned, (1, 3))
    outgoing(sums, turned, swap, place[0], 1, near_a, near_b)


def back_kernel(place, grad, grad_b, grad_a, weight, total, lhs):
    swap = exchange_matrix()
    spot = place[0]
    even = lax.rem(spot, 2) == 0
    lhs[1, :ROWS] = grad[...]
    for tile in range(COUT // TILE):
        span = slice(tile * TILE, (tile + 1) * TILE)
        lhs[1, ROWS:, span] = flip_tile(grad, tile, COUT // TILE, swap).astype(BF)
    stack_pair(lhs, even, spot + 1 < 8, spot - 1 >= 0, grad_a, grad_b, 0, 2, swap)
    for part in range(CH // PART_OUT):
        span = slice(part * PART_OUT, (part + 1) * PART_OUT)
        total[:, span] = (
            pull_back(lhs[0], weight[1, span])
            + pull_back(lhs[1], weight[2, span])
            + pull_back(lhs[2], weight[3, span])
        )


def relay_kernel(near_a, near_b, from_a, from_b, to_a, to_b):
    to_a[...] = (near_a[...] + from_b[...].astype(F32)).astype(BF)
    to_b[...] = (near_b[...] + from_a[...].astype(F32)).astype(BF)


def join_kernel(own, from_a, from_b, terms, convolved, gain_grad):
    convolved[...] = (own[...] + (from_a[...].astype(F32) + from_b[...].astype(F32))).astype(BF)
    gain_grad[...] = jnp.sum(terms[...], axis=0) * (1.0 / math.sqrt(2 * 16384))


def stack_pair(lhs, even, ok_ahead, ok_behind, first, second, tap_low, tap_high, swap):
    zero = jnp.zeros((ROWS, COUT), BF)
    for flag, ahead_ref, behind_ref in ((True, first, second), (False, second, first)):

        @pl.when(even if flag else jnp.logical_not(even))
        def _(ahead_ref=ahead_ref, behind_ref=behind_ref):
            lhs[tap_low, :ROWS] = jnp.where(ok_ahead, ahead_ref[...], zero)
            lhs[tap_high, :ROWS] = jnp.where(ok_behind, behind_ref[...], zero)

    for tile in range(COUT // TILE):
        span = slice(tile * TILE, (tile + 1) * TILE)
        lhs[tap_low, ROWS:, span] = flip_tile(lhs.at[tap_high], tile, COUT // TILE, swap, slice(0, ROWS)).astype(BF)
        lhs[tap_high, ROWS:, span] = flip_tile(lhs.at[tap_low], tile, COUT // TILE, swap, slice(0, ROWS)).astype(BF)


def pull_back(rows, weight):
    return lax.dot_general(rows, weight, (((1,), (1,)), ((), ())), preferred_element_type=F32)


def last_kernel(place, from_b, from_a, held, near, normed, gain, slope, inv_rms, grad, gain_part, total, lhs, turned):
    swap = exchange_matrix()
    spot = place[0]
    even = lax.rem(spot, 2) == 0
    stack_pair(lhs, even, spot + 2 < 8, spot - 2 >= 0, from_a, from_b, 0, 1, swap)
    for part in range(CH // PART_OUT):
        span = slice(part * PART_OUT, (part + 1) * PART_OUT)
        term = near[:, span] + pull_back(lhs[0], held[0, span]) + pull_back(lhs[1], held[1, span])
        total[:, span] = term[:ROWS]
        turned[:, span] = term[ROWS:].astype(BF)
    spread = jnp.zeros((ROWS, 1), F32)
    for tile in range(CH // TILE):
        flipped = flip_tile(turned, tile, CH // TILE, swap)
        for half in range(TILE // LANES):
            lane = tile * (TILE // LANES) + half
            span = slice(lane * LANES, (lane + 1) * LANES)
            hidden_grad = total[:, span] + flipped[:, half * LANES : (half + 1) * LANES]
            scaled_grad = hidden_grad * slope[:, span]
            product = scaled_grad * normed[:, span]
            gain_part[:, lane : lane + 1] = jnp.broadcast_to(jnp.sum(product, axis=0, keepdims=True)[None], (GROUP, 1, LANES))
            spread = spread + jnp.sum(product * gain[lane : lane + 1], axis=-1, keepdims=True)
            total[:, span] = scaled_grad * gain[lane : lane + 1]
    spread = spread * (1.0 / CH)
    scale = inv_rms[...]
    for tile in range(CH // TILE):
        span = slice(tile * TILE, (tile + 1) * TILE)
        grad[:, span] = (scale * (total[:, span] - normed[:, span] * spread)).astype(BF)


VMEM = pl.BlockSpec(memory_space=pltpu.VMEM)
SMEM = pl.BlockSpec(memory_space=pltpu.SMEM)
HBM = pl.BlockSpec(memory_space=pl.ANY)
LIMIT = pltpu.CompilerParams(vmem_limit_bytes=24 * 2**20)


def shape(dims, kind):
    return jax.ShapeDtypeStruct(dims, kind)


def remote(value):
    return pltpu.with_memory_space_constraint(value, pltpu.HBM)


def local(value):
    return pltpu.with_memory_space_constraint(value, pltpu.VMEM)


def first(place, features, gain, weight):
    return pl.pallas_call(
        first_kernel,
        out_shape=(
            pltpu.VMEM((2, CH, COUT), BF),
            pltpu.VMEM((2 * ROWS, CH), BF),
            pltpu.VMEM((ROWS, CH), F32),
            pltpu.VMEM((ROWS, CH), F32),
            pltpu.VMEM((ROWS, 1), F32),
            pltpu.VMEM((ROWS, COUT), BF),
            pltpu.VMEM((ROWS, COUT), BF),
            pltpu.VMEM((CH // LANES, LANES), F32),
        ),
        in_specs=[SMEM, HBM, HBM, HBM],
        out_specs=[VMEM] * 8,
        scratch_shapes=[
            pltpu.VMEM((ROWS, CH), BF),
            pltpu.VMEM((2, ROWS, COUT), F32),
            pltpu.VMEM((2, ROWS, COUT), BF),
            pltpu.SemaphoreType.DMA,
            pltpu.SemaphoreType.DMA,
            pltpu.SemaphoreType.DMA((2, PARTS)),
        ],
        compiler_params=LIMIT,
        cost_estimate=pl.CostEstimate(flops=1300000000, bytes_accessed=6000000, transcendentals=200000),
        name="first",
    )(place, remote(features), remote(gain), remote(weight))


def ahead(place, stacked, weight):
    return pl.pallas_call(
        ahead_kernel,
        out_shape=(
            pltpu.VMEM((ROWS, COUT), F32),
            pltpu.VMEM((ROWS, COUT), F32),
            pltpu.VMEM((ROWS, COUT), F32),
        ),
        in_specs=[SMEM] + [VMEM] * 2,
        out_specs=[VMEM] * 3,
        scratch_shapes=[
            pltpu.VMEM((2, ROWS, COUT), F32),
            pltpu.VMEM((2, ROWS, COUT), BF),
        ],
        compiler_params=LIMIT,
        cost_estimate=pl.CostEstimate(flops=1800000000, bytes_accessed=1000000, transcendentals=0),
        name="ahead",
    )(place, local(stacked), local(weight))


def back(place, grad, grad_b, grad_a, weight):
    return pl.pallas_call(
        back_kernel,
        out_shape=pltpu.VMEM((2 * ROWS, CH), F32),
        in_specs=[SMEM] + [VMEM] * 4,
        out_specs=VMEM,
        scratch_shapes=[pltpu.VMEM((3, 2 * ROWS, COUT), BF)],
        compiler_params=LIMIT,
        cost_estimate=pl.CostEstimate(flops=1800000000, bytes_accessed=1000000, transcendentals=0),
        name="back",
    )(place, *(local(value) for value in (grad, grad_b, grad_a, weight)))


def last(place, from_b, from_a, held, near, normed, gain, slope, inv_rms):
    return pl.pallas_call(
        last_kernel,
        out_shape=(shape((ROWS, CH), BF), pltpu.VMEM((GROUP, CH // LANES, LANES), F32)),
        in_specs=[SMEM] + [VMEM] * 8,
        out_specs=[VMEM] * 2,
        scratch_shapes=[
            pltpu.VMEM((ROWS, CH), F32),
            pltpu.VMEM((2, 2 * ROWS, COUT), BF),
            pltpu.VMEM((ROWS, CH), BF),
        ],
        compiler_params=LIMIT,
        cost_estimate=pl.CostEstimate(flops=1300000000, bytes_accessed=1000000, transcendentals=0),
        name="last",
    )(place, *(local(value) for value in (from_b, from_a, held, near, normed, gain, slope, inv_rms)))


def relay(near_a, near_b, from_a, from_b):
    return pl.pallas_call(
        relay_kernel,
        out_shape=(pltpu.VMEM((ROWS, COUT), BF), pltpu.VMEM((ROWS, COUT), BF)),
        in_specs=[VMEM] * 4,
        out_specs=[VMEM] * 2,
        compiler_params=LIMIT,
        cost_estimate=pl.CostEstimate(flops=400000, bytes_accessed=1000000, transcendentals=0),
        name="relay",
    )(local(near_a), local(near_b), local(from_a), local(from_b))


def join(*values):
    return pl.pallas_call(
        join_kernel,
        out_shape=(shape((ROWS, COUT), BF), shape((CH // LANES, LANES), F32)),
        in_specs=[VMEM] * 4,
        out_specs=[VMEM] * 2,
        compiler_params=LIMIT,
        cost_estimate=pl.CostEstimate(flops=200000, bytes_accessed=1000000, transcendentals=0),
        name="join",
    )(*(local(value) for value in values))


def collect_kernel(terms, copies):
    copies[...] = jnp.broadcast_to(jnp.sum(terms[...], axis=0, keepdims=True), copies.shape)


def collect(terms):
    return pl.pallas_call(
        collect_kernel,
        out_shape=pltpu.VMEM((GROUP, CH // LANES, LANES), F32),
        in_specs=[VMEM],
        out_specs=VMEM,
        compiler_params=LIMIT,
        cost_estimate=pl.CostEstimate(flops=30000, bytes_accessed=200000, transcendentals=0),
        name="collect",
    )(local(terms))


def exchange_a(value):
    return lax.ppermute(value, "ctx", [(i, ((i // 16) ^ 1) * 16 + i % 16) for i in range(128)])


def exchange_b(value):
    pairs = []
    for i in range(128):
        spot = i // 16
        if spot in (0, 7):
            pairs.append((i, i ^ 1))
        else:
            other = spot + 1 if spot % 2 else spot - 1
            pairs.append((i, other * 16 + i % 16))
    return lax.ppermute(value, "ctx", pairs)


BOTH = ("dp", "ctx")


def trade(copies, groups):
    return lax.all_to_all(copies, BOTH, 0, 0, axis_index_groups=groups, tiled=True)


def sum_everywhere(copies):
    terms = trade(copies, [list(range(first, first + GROUP)) for first in range(0, 256, GROUP)])
    return trade(collect(terms), [list(range(first, 256, GROUP)) for first in range(GROUP)])


def per_device(features, gain, conv_weight, cotangent):
    spot = (lax.axis_index("ctx") // 16).astype(jnp.int32)
    place = spot.reshape(1)
    rows = features.reshape(ROWS, CH)
    gains = gain.reshape(CH // LANES, LANES)
    own = cotangent.reshape(ROWS, COUT)
    grad_b = exchange_b(own)
    grad_a = exchange_a(own)
    held, stacked, normed, slope, inv_rms, far_a, far_b, gain_rows = first(place, rows, gains, conv_weight)
    grad_a, held, stacked = lax.optimization_barrier((grad_a, held, stacked))
    grad_ab = exchange_b(grad_a)
    near_a, near_b, center = ahead(place, stacked, conv_weight)
    grad_b, center = lax.optimization_barrier((grad_b, center))
    grad_ba = exchange_a(grad_b)
    near = back(place, own, grad_b, grad_a, conv_weight)
    input_grad, gain_part = last(place, grad_ab, grad_ba, held, near, normed, gain_rows, slope, inv_rms)
    to_a, to_b = relay(near_a, near_b, exchange_a(far_a), exchange_b(far_b))
    terms = sum_everywhere(gain_part)
    convolved, gain_grad = join(center, exchange_a(to_a), exchange_b(to_b), terms)
    return (
        convolved.reshape(1, ROWS, COUT),
        input_grad.reshape(1, ROWS, CH),
        gain_grad.reshape(CH),
    )


def solution(mesh):
    return jax.shard_map(
        per_device,
        mesh=mesh,
        in_specs=(P("dp", "ctx", None), P(), P(), P("dp", "ctx", None)),
        out_specs=(P("dp", "ctx", None), P("dp", "ctx", None), P()),
        check_vma=False,
    )
```

```python
import math

import jax
import jax.numpy as jnp
from jax import lax
from jax.experimental import pallas as pl
from jax.experimental.pallas import tpu as pltpu
from jax.sharding import PartitionSpec as P

TAPS = 5
EPS = 1e-06
ROWS = 128
CH = 1536
COUT = 768
TILE = 256
ROOT = math.sqrt(2.0 / math.pi)
CUBE = 0.044715
LANES = 128
GROUP = 16
PART_OUT = 512
BF = jnp.bfloat16
F32 = jnp.float32


def exchange_matrix():
    rows = lax.broadcasted_iota(jnp.int32, (TILE, TILE), 0)
    cols = lax.broadcasted_iota(jnp.int32, (TILE, TILE), 1)
    return jnp.where(rows + cols == TILE - 1, 1.0, 0.0).astype(BF)


def flip_tile(ref, tile, count, swap, rows=slice(None)):
    first = (count - 1 - tile) * TILE
    return jnp.dot(ref[rows, first : first + TILE], swap, preferred_element_type=F32)


def partial_sums(stacked, held, sums, turned, slots):
    for place, slot in enumerate(slots):
        product = jnp.dot(stacked[...], held[slot], preferred_element_type=F32)
        sums[place] = product[:ROWS]
        turned[place] = product[ROWS:].astype(BF)


def outgoing(sums, turned, swap, spot, reach, to_a, to_b):
    even = lax.rem(spot, 2) == 0
    ahead_ok = spot + reach < 8
    behind_ok = spot - reach >= 0
    for tile in range(COUT // TILE):
        span = slice(tile * TILE, (tile + 1) * TILE)
        ahead = sums[0, :, span] + flip_tile(turned.at[1], tile, COUT // TILE, swap)
        behind = sums[1, :, span] + flip_tile(turned.at[0], tile, COUT // TILE, swap)
        ahead = jnp.where(ahead_ok, ahead, 0.0)
        behind = jnp.where(behind_ok, behind, 0.0)
        to_a[:, span] = jnp.where(even, ahead, behind).astype(to_a.dtype)
        to_b[:, span] = jnp.where(even, behind, ahead).astype(to_b.dtype)


def first_kernel(source, gain_source, stacked, normed, slope, inv_rms, gain, features, row_sem, gain_sem):
    load = pltpu.make_async_copy(source, features, row_sem)
    load.start()
    gain_load = pltpu.make_async_copy(gain_source, gain, gain_sem)
    gain_load.start()
    swap = exchange_matrix()
    load.wait()
    wide = features[...].astype(F32)
    scale = lax.rsqrt(jnp.mean(wide * wide, axis=-1, keepdims=True) + EPS)
    inv_rms[...] = scale
    gain_load.wait()
    for lane in range(CH // LANES):
        span = slice(lane * LANES, (lane + 1) * LANES)
        value = features[:, span].astype(F32) * scale
        normed[:, span] = value
        scaled = value * gain[lane : lane + 1]
        square = scaled * scaled
        bend = jnp.tanh(ROOT * (scaled + CUBE * (square * scaled)))
        stacked[:ROWS, span] = (0.5 * scaled * (1.0 + bend)).astype(BF)
        slope[:, span] = 0.5 * (1.0 + bend) + 0.5 * scaled * (1.0 - bend * bend) * (
            ROOT * (1.0 + 3.0 * CUBE * square)
        )
    for tile in range(CH // TILE):
        span = slice(tile * TILE, (tile + 1) * TILE)
        stacked[ROWS:, span] = flip_tile(stacked, tile, CH // TILE, swap, slice(0, ROWS)).astype(BF)


def ahead_kernel(place, stacked, weight, far_a, far_b, near_a, near_b, own, sums, turned):
    swap = exchange_matrix()
    partial_sums(stacked, weight, sums, turned, (0, 4))
    outgoing(sums, turned, swap, place[0], 2, far_a, far_b)
    partial_sums(stacked, weight, sums, turned, (2,))
    for tile in range(COUT // TILE):
        span = slice(tile * TILE, (tile + 1) * TILE)
        own[:, span] = sums[0, :, span] + flip_tile(turned.at[0], tile, COUT // TILE, swap)
    partial_sums(stacked, weight, sums, turned, (1, 3))
    outgoing(sums, turned, swap, place[0], 1, near_a, near_b)


def back_kernel(place, grad, grad_b, grad_a, weight, total, lhs):
    swap = exchange_matrix()
    spot = place[0]
    even = lax.rem(spot, 2) == 0
    lhs[1, :ROWS] = grad[...]
    for tile in range(COUT // TILE):
        span = slice(tile * TILE, (tile + 1) * TILE)
        lhs[1, ROWS:, span] = flip_tile(grad, tile, COUT // TILE, swap).astype(BF)
    stack_pair(lhs, even, spot + 1 < 8, spot - 1 >= 0, grad_a, grad_b, 0, 2, swap)
    for part in range(CH // PART_OUT):
        span = slice(part * PART_OUT, (part + 1) * PART_OUT)
        total[:, span] = (
            pull_back(lhs[0], weight[1, span])
            + pull_back(lhs[1], weight[2, span])
            + pull_back(lhs[2], weight[3, span])
        )


def relay_kernel(near_a, near_b, from_a, from_b, to_a, to_b):
    to_a[...] = (near_a[...] + from_b[...].astype(F32)).astype(BF)
    to_b[...] = (near_b[...] + from_a[...].astype(F32)).astype(BF)


def join_kernel(own, from_a, from_b, terms, convolved, gain_grad):
    convolved[...] = (own[...] + (from_a[...].astype(F32) + from_b[...].astype(F32))).astype(BF)
    gain_grad[...] = jnp.sum(terms[...], axis=0) * (1.0 / math.sqrt(2 * 16384))


def stack_pair(lhs, even, ok_ahead, ok_behind, first, second, tap_low, tap_high, swap):
    zero = jnp.zeros((ROWS, COUT), BF)
    for flag, ahead_ref, behind_ref in ((True, first, second), (False, second, first)):

        @pl.when(even if flag else jnp.logical_not(even))
        def _(ahead_ref=ahead_ref, behind_ref=behind_ref):
            lhs[tap_low, :ROWS] = jnp.where(ok_ahead, ahead_ref[...], zero)
            lhs[tap_high, :ROWS] = jnp.where(ok_behind, behind_ref[...], zero)

    for tile in range(COUT // TILE):
        span = slice(tile * TILE, (tile + 1) * TILE)
        lhs[tap_low, ROWS:, span] = flip_tile(lhs.at[tap_high], tile, COUT // TILE, swap, slice(0, ROWS)).astype(BF)
        lhs[tap_high, ROWS:, span] = flip_tile(lhs.at[tap_low], tile, COUT // TILE, swap, slice(0, ROWS)).astype(BF)


def pull_back(rows, weight):
    return lax.dot_general(rows, weight, (((1,), (1,)), ((), ())), preferred_element_type=F32)


def last_kernel(place, from_b, from_a, held, near, normed, gain, slope, inv_rms, grad, gain_part, total, lhs, turned):
    swap = exchange_matrix()
    spot = place[0]
    even = lax.rem(spot, 2) == 0
    stack_pair(lhs, even, spot + 2 < 8, spot - 2 >= 0, from_a, from_b, 0, 1, swap)
    for part in range(CH // PART_OUT):
        span = slice(part * PART_OUT, (part + 1) * PART_OUT)
        term = near[:, span] + pull_back(lhs[0], held[0, span]) + pull_back(lhs[1], held[4, span])
        total[:, span] = term[:ROWS]
        turned[:, span] = term[ROWS:].astype(BF)
    spread = jnp.zeros((ROWS, 1), F32)
    for tile in range(CH // TILE):
        flipped = flip_tile(turned, tile, CH // TILE, swap)
        for half in range(TILE // LANES):
            lane = tile * (TILE // LANES) + half
            span = slice(lane * LANES, (lane + 1) * LANES)
            hidden_grad = total[:, span] + flipped[:, half * LANES : (half + 1) * LANES]
            scaled_grad = hidden_grad * slope[:, span]
            product = scaled_grad * normed[:, span]
            gain_part[:, lane : lane + 1] = jnp.broadcast_to(jnp.sum(product, axis=0, keepdims=True)[None], (GROUP, 1, LANES))
            spread = spread + jnp.sum(product * gain[lane : lane + 1], axis=-1, keepdims=True)
            total[:, span] = scaled_grad * gain[lane : lane + 1]
    spread = spread * (1.0 / CH)
    scale = inv_rms[...]
    for tile in range(CH // TILE):
        span = slice(tile * TILE, (tile + 1) * TILE)
        grad[:, span] = (scale * (total[:, span] - normed[:, span] * spread)).astype(BF)


VMEM = pl.BlockSpec(memory_space=pltpu.VMEM)
SMEM = pl.BlockSpec(memory_space=pltpu.SMEM)
HBM = pl.BlockSpec(memory_space=pl.ANY)
LIMIT = pltpu.CompilerParams(vmem_limit_bytes=24 * 2**20)


def shape(dims, kind):
    return jax.ShapeDtypeStruct(dims, kind)


def remote(value):
    return pltpu.with_memory_space_constraint(value, pltpu.HBM)


def local(value):
    return pltpu.with_memory_space_constraint(value, pltpu.VMEM)


def first(features, gain):
    return pl.pallas_call(
        first_kernel,
        out_shape=(
            pltpu.VMEM((2 * ROWS, CH), BF),
            pltpu.VMEM((ROWS, CH), F32),
            pltpu.VMEM((ROWS, CH), F32),
            pltpu.VMEM((ROWS, 1), F32),
            pltpu.VMEM((CH // LANES, LANES), F32),
        ),
        in_specs=[HBM] * 2,
        out_specs=[VMEM] * 5,
        scratch_shapes=[pltpu.VMEM((ROWS, CH), BF), pltpu.SemaphoreType.DMA, pltpu.SemaphoreType.DMA],
        compiler_params=LIMIT,
        cost_estimate=pl.CostEstimate(flops=5000000, bytes_accessed=6000000, transcendentals=200000),
        name="first",
    )(remote(features), remote(gain))


def ahead(place, stacked, weight):
    return pl.pallas_call(
        ahead_kernel,
        out_shape=(
            pltpu.VMEM((ROWS, COUT), BF),
            pltpu.VMEM((ROWS, COUT), BF),
            pltpu.VMEM((ROWS, COUT), F32),
            pltpu.VMEM((ROWS, COUT), F32),
            pltpu.VMEM((ROWS, COUT), F32),
        ),
        in_specs=[SMEM] + [VMEM] * 2,
        out_specs=[VMEM] * 5,
        scratch_shapes=[
            pltpu.VMEM((2, ROWS, COUT), F32),
            pltpu.VMEM((2, ROWS, COUT), BF),
        ],
        compiler_params=LIMIT,
        cost_estimate=pl.CostEstimate(flops=3000000000, bytes_accessed=1000000, transcendentals=0),
        name="ahead",
    )(place, local(stacked), local(weight))


def back(place, grad, grad_b, grad_a, weight):
    return pl.pallas_call(
        back_kernel,
        out_shape=pltpu.VMEM((2 * ROWS, CH), F32),
        in_specs=[SMEM] + [VMEM] * 4,
        out_specs=VMEM,
        scratch_shapes=[pltpu.VMEM((3, 2 * ROWS, COUT), BF)],
        compiler_params=LIMIT,
        cost_estimate=pl.CostEstimate(flops=1800000000, bytes_accessed=1000000, transcendentals=0),
        name="back",
    )(place, *(local(value) for value in (grad, grad_b, grad_a, weight)))


def last(place, from_b, from_a, held, near, normed, gain, slope, inv_rms):
    return pl.pallas_call(
        last_kernel,
        out_shape=(shape((ROWS, CH), BF), pltpu.VMEM((GROUP, CH // LANES, LANES), F32)),
        in_specs=[SMEM] + [VMEM] * 8,
        out_specs=[VMEM] * 2,
        scratch_shapes=[
            pltpu.VMEM((ROWS, CH), F32),
            pltpu.VMEM((2, 2 * ROWS, COUT), BF),
            pltpu.VMEM((ROWS, CH), BF),
        ],
        compiler_params=LIMIT,
        cost_estimate=pl.CostEstimate(flops=1300000000, bytes_accessed=1000000, transcendentals=0),
        name="last",
    )(place, *(local(value) for value in (from_b, from_a, held, near, normed, gain, slope, inv_rms)))


def relay(near_a, near_b, from_a, from_b):
    return pl.pallas_call(
        relay_kernel,
        out_shape=(pltpu.VMEM((ROWS, COUT), BF), pltpu.VMEM((ROWS, COUT), BF)),
        in_specs=[VMEM] * 4,
        out_specs=[VMEM] * 2,
        compiler_params=LIMIT,
        cost_estimate=pl.CostEstimate(flops=400000, bytes_accessed=1000000, transcendentals=0),
        name="relay",
    )(local(near_a), local(near_b), local(from_a), local(from_b))


def join(*values):
    return pl.pallas_call(
        join_kernel,
        out_shape=(shape((ROWS, COUT), BF), shape((CH // LANES, LANES), F32)),
        in_specs=[VMEM] * 4,
        out_specs=[VMEM] * 2,
        compiler_params=LIMIT,
        cost_estimate=pl.CostEstimate(flops=200000, bytes_accessed=1000000, transcendentals=0),
        name="join",
    )(*(local(value) for value in values))


def collect_kernel(terms, copies):
    copies[...] = jnp.broadcast_to(jnp.sum(terms[...], axis=0, keepdims=True), copies.shape)


def collect(terms):
    return pl.pallas_call(
        collect_kernel,
        out_shape=pltpu.VMEM((GROUP, CH // LANES, LANES), F32),
        in_specs=[VMEM],
        out_specs=VMEM,
        compiler_params=LIMIT,
        cost_estimate=pl.CostEstimate(flops=30000, bytes_accessed=200000, transcendentals=0),
        name="collect",
    )(local(terms))


def exchange_a(value):
    return lax.ppermute(value, "ctx", [(i, ((i // 16) ^ 1) * 16 + i % 16) for i in range(128)])


def exchange_b(value):
    pairs = []
    for i in range(128):
        spot = i // 16
        if spot in (0, 7):
            pairs.append((i, i ^ 1))
        else:
            other = spot + 1 if spot % 2 else spot - 1
            pairs.append((i, other * 16 + i % 16))
    return lax.ppermute(value, "ctx", pairs)


BOTH = ("dp", "ctx")


def trade(copies, groups):
    return lax.all_to_all(copies, BOTH, 0, 0, axis_index_groups=groups, tiled=True)


def sum_everywhere(copies):
    terms = trade(copies, [list(range(first, first + GROUP)) for first in range(0, 256, GROUP)])
    return trade(collect(terms), [list(range(first, 256, GROUP)) for first in range(GROUP)])


def per_device(features, gain, conv_weight, cotangent):
    spot = (lax.axis_index("ctx") // 16).astype(jnp.int32)
    place = spot.reshape(1)
    rows = features.reshape(ROWS, CH)
    gains = gain.reshape(CH // LANES, LANES)
    own = cotangent.reshape(ROWS, COUT)
    grad_b = exchange_b(own)
    grad_a = exchange_a(own)
    stacked, normed, slope, inv_rms, gain_rows = first(rows, gains)
    grad_a, stacked = lax.optimization_barrier((grad_a, stacked))
    grad_ab = exchange_b(grad_a)
    far_a, far_b, near_a, near_b, center = ahead(place, stacked, conv_weight)
    grad_b, center = lax.optimization_barrier((grad_b, center))
    grad_ba = exchange_a(grad_b)
    near = back(place, own, grad_b, grad_a, conv_weight)
    input_grad, gain_part = last(place, grad_ab, grad_ba, conv_weight, near, normed, gain_rows, slope, inv_rms)
    to_a, to_b = relay(near_a, near_b, exchange_a(far_a), exchange_b(far_b))
    terms = sum_everywhere(gain_part)
    convolved, gain_grad = join(center, exchange_a(to_a), exchange_b(to_b), terms)
    return (
        convolved.reshape(1, ROWS, COUT),
        input_grad.reshape(1, ROWS, CH),
        gain_grad.reshape(CH),
    )


def solution(mesh):
    return jax.shard_map(
        per_device,
        mesh=mesh,
        in_specs=(P("dp", "ctx", None), P(), P(), P("dp", "ctx", None)),
        out_specs=(P("dp", "ctx", None), P("dp", "ctx", None), P()),
        check_vma=False,
    )
```
